32 devices in a mesh: space: 8 (over z, x), dir: 4 (over y, core).
Axes of the slice: x: 2, y: 2, z: 4, core: 2. Of those that a mesh axis runs over, the one named last changes fastest.
Arguments:
- incident: float32 [2, 128, 32768], P(None, 'dir', 'space'), may hold values from -6 to 6
- pair_blocks: bfloat16 [768, 2, 128, 128], P('space'), may hold values from -0.046875 to 0.046875
- pair_local: int32 [768], P('space'), may hold values from 0 to 31, as said below
- pair_partner: int32 [768], P('space'), may hold values from 0 to 255, as said below
- pair_count: int32 [8], P('space'), may hold values from 32 to 64, as said below
- self_blocks: bfloat16 [256, 2, 128, 128], P('space'), may hold values from -0.046875 to 0.046875
- far_in: bfloat16 [256, 2, 32, 128], P('space'), may hold values from -0.5 to 0.5
- far_out: bfloat16 [256, 2, 32, 128], P('space'), may hold values from -0.046875 to 0.046875
- far_rank: int32 [256], P('space'), may hold values from 8 to 32
Outputs:
- solution: float32 [2, 128, 32768], P(None, 'dir', 'space')
- intensity: float32 [32768], P('space')
The draws below stay inside these ranges and needn't reach their ends.
Inputs may be any that keep to these rules, and one draw needn't show every extreme that they name: `pair_local`: local cluster of a pair, from 0 to 31. For the first 32 slots of each index of space the partner lies on the index just before or just after, within 8 clusters of the shared boundary, and the local cluster lies within 8 clusters of that same boundary; on every index that has a neighbour on a side, some pair names that neighbour's cluster farthest from the boundary within that reach. All other slots pair two different clusters of the same index. Pairs may repeat. `pair_partner`: global cluster number of a pair's partner, as described for pair_local. Slots 32 + pair_count[o] to 95 of index o are empty; some index is full in every draw.
All inputs are finite; a program needn't handle non-finite values.
Results may differ from the reference program's by a relative error of at most 0.003.
Values may be sent and summed in bfloat16 or wider, within the bound.
A program may use at most 128 MiB of HBM per device.

```python
import jax
import jax.numpy as jnp
from jax import lax

P_SIZE = 128
NDIR = 128
R = 32
ITERS = 3
CL_DEV = 32
NP_DEV = 96
REMOTE_DEV = 32
RIM = 8
CLUSTERS = 256
NPAN = 32768
NPAIRS = 768
N_SPACE = 8


def pair_tables(key):
    count_dev = CLUSTERS // CL_DEV
    keys = jax.random.split(key, 4)
    index = jnp.arange(NPAIRS, dtype=jnp.int32)
    owner = index // NP_DEV
    slot = index % NP_DEV
    half = REMOTE_DEV // 2
    side = jnp.where(slot < half, -1, 1)
    side = jnp.where(owner == 0, 1, side)
    side = jnp.where(owner == count_dev - 1, -1, side)
    offset_i = jax.random.randint(keys[0], (NPAIRS,), 0, RIM)
    offset_j = jax.random.randint(keys[1], (NPAIRS,), 0, RIM)
    offset_j = jnp.where((slot == 0) | (slot == half), 0, offset_j)
    remote_local = jnp.where(side < 0, offset_i, CL_DEV - 1 - offset_i)
    remote_partner = jnp.where(side < 0, owner * CL_DEV - RIM + offset_j, owner * CL_DEV + CL_DEV + RIM - 1 - offset_j)
    near_local = jax.random.randint(keys[2], (NPAIRS,), 0, CL_DEV)
    stride = jax.random.randint(keys[3], (NPAIRS,), 1, CL_DEV)
    near_partner = owner * CL_DEV + (near_local + stride) % CL_DEV
    remote = slot < REMOTE_DEV
    local = jnp.where(remote, remote_local, near_local).astype(jnp.int32)
    partner = jnp.where(remote, remote_partner, near_partner).astype(jnp.int32)
    return (local, partner)


def draw_pair_local(key, part):
    local, partner = pair_tables(key)
    return local


def draw_pair_partner(key, part):
    local, partner = pair_tables(key)
    return partner


def draw_pair_count(key, part):
    key = jax.random.fold_in(key, 7)
    count_dev = CLUSTERS // CL_DEV
    first, second = jax.random.split(key)
    full = NP_DEV - REMOTE_DEV
    counts = jax.random.randint(first, (count_dev,), full // 2, full + 1)
    chosen = jax.random.randint(second, (), 0, count_dev)
    counts = jnp.where(jnp.arange(count_dev) == chosen, full, counts)
    return counts.astype(jnp.int32)


def plant(entries, key, least, high):
    place = [jax.random.randint(jax.random.fold_in(key, axis), (), 0, length) for axis, length in enumerate(entries.shape)]
    widest = entries.shape.index(max(entries.shape))
    neighbour = place[:widest] + [(place[widest] + 1) % entries.shape[widest]] + place[widest + 1:]
    return entries.at[tuple(place)].set(least).at[tuple(neighbour)].set(high)


def steps_of(own_key, extent, cuts, least, high):
    def one(position, blocks):
        heights = jax.random.uniform(jax.random.fold_in(jax.random.fold_in(own_key, 6), position), (blocks,), jnp.float32, least / len(cuts), high / len(cuts))
        return jnp.repeat(jnp.exp(heights), extent[position] // blocks).reshape((-1,) + (1,) * (len(extent) - position - 1))

    level = one(*cuts[0])
    for cut in cuts[1:]:
        level = level * one(*cut)
    return level


def scatter_about(stream_key, extent, width, limit, cuts=(), kind=jnp.bfloat16):
    values = jax.random.normal(stream_key, extent, jnp.float32) * width
    if len(cuts) > 0:
        values = steps_of(stream_key, extent, cuts, -0.22, 0.18) * values
    return jnp.clip(values, min=-limit, max=limit).astype(kind)


def setup_inputs(seed: int = 0) -> dict:
    streams_of = jax.random.split(jax.random.key(seed), 10)
    return {
        "incident": scatter_about(streams_of[0], (2, NDIR, NPAN), 1.0, 6.0, ((1, 4), (2, 8)), jnp.float32),
        "pair_blocks": scatter_about(streams_of[1], (NPAIRS, 2, P_SIZE, P_SIZE), (128 * P_SIZE) ** -0.5, 0.046875, ((0, 8),)),
        "pair_local": draw_pair_local(jax.random.fold_in(streams_of[9], 71), 0),
        "pair_partner": draw_pair_partner(jax.random.fold_in(streams_of[9], 71), 0),
        "pair_count": draw_pair_count(jax.random.fold_in(streams_of[9], 71), 0),
        "self_blocks": scatter_about(streams_of[5], (CLUSTERS, 2, P_SIZE, P_SIZE), (128 * P_SIZE) ** -0.5, 0.046875, ((0, 8),)),
        "far_in": scatter_about(streams_of[6], (CLUSTERS, 2, R, P_SIZE), P_SIZE ** -0.5, 0.5, ((0, 8),)),
        "far_out": scatter_about(streams_of[7], (CLUSTERS, 2, R, P_SIZE), (2 * CLUSTERS * R) ** -0.5, 0.046875, ((0, 8),)),
        "far_rank": plant(jax.random.randint(streams_of[8], (CLUSTERS,), R // 4, R + 1), jax.random.fold_in(streams_of[8], 1), R // 4, R).astype(jnp.int32),
    }


def complex_product(spec, blocks, vec):

    def one(left, right):
        return jnp.einsum(spec, left.astype(jnp.float32), right.astype(jnp.float32))
    real = one(blocks[:, 0], vec[0]) - one(blocks[:, 1], vec[1])
    imag = one(blocks[:, 0], vec[1]) + one(blocks[:, 1], vec[0])
    return jnp.stack([real, imag])

def inner(first, second):
    real = lax.optimization_barrier(jnp.sum(first[0] * second[0] + first[1] * second[1], axis=(1, 2)))
    imag = lax.optimization_barrier(jnp.sum(first[0] * second[1] - first[1] * second[0], axis=(1, 2)))
    return jnp.stack([real, imag])

def scale_by(factor, vec):
    fr = factor[0][:, None, None]
    fi = factor[1][:, None, None]
    return jnp.stack([fr * vec[0] - fi * vec[1], fr * vec[1] + fi * vec[0]])

def solve_small(matrix, vector):
    order = len(vector)
    rows = [list(line) for line in matrix]
    values = list(vector)
    for col in range(order):
        for row in range(col + 1, order):
            factor = rows[row][col] / rows[col][col]
            for other in range(col, order):
                rows[row][other] = rows[row][other] - factor * rows[col][other]
            values[row] = values[row] - factor * values[col]
    result = [None] * order
    for row in range(order - 1, -1, -1):
        total = values[row]
        for other in range(row + 1, order):
            total = total - rows[row][other] * result[other]
        result[row] = total / rows[row][row]
    return result

def least_squares(hess, beta):
    count = len(hess[0])
    g_real = [[None] * count for _ in range(count)]
    g_imag = [[None] * count for _ in range(count)]
    for first in range(count):
        for second in range(count):
            total_r = 0.0
            total_i = 0.0
            for row in range(count + 1):
                ha = hess[row][first]
                hb = hess[row][second]
                total_r = total_r + ha[0] * hb[0] + ha[1] * hb[1]
                total_i = total_i + ha[0] * hb[1] - ha[1] * hb[0]
            g_real[first][second] = total_r
            g_imag[first][second] = total_i
    matrix = []
    for first in range(count):
        matrix.append([g_real[first][b] for b in range(count)] + [-g_imag[first][b] for b in range(count)])
    for first in range(count):
        matrix.append([g_imag[first][b] for b in range(count)] + [g_real[first][b] for b in range(count)])
    vector = [beta * hess[0][a][0] for a in range(count)] + [-beta * hess[0][a][1] for a in range(count)]
    found = solve_small(matrix, vector)
    return [jnp.stack([found[a], found[a + count]]) for a in range(count)]

def reference(incident, pair_blocks, pair_local, pair_partner, pair_count, self_blocks, far_in, far_out, far_rank):
    slots = jnp.arange(NP_DEV, dtype=jnp.int32)
    ranks_axis = jnp.arange(R, dtype=jnp.int32)
    owners = jnp.arange(N_SPACE, dtype=jnp.int32)

    def operate(vec):
        rounded = lax.optimization_barrier(vec.astype(jnp.bfloat16))

        def step(carry, owner):
            total, moments = carry
            blocks = lax.dynamic_slice_in_dim(pair_blocks, owner * NP_DEV, NP_DEV, 0)
            local = lax.dynamic_slice_in_dim(pair_local, owner * NP_DEV, NP_DEV, 0) + owner * CL_DEV
            partner = lax.dynamic_slice_in_dim(pair_partner, owner * NP_DEV, NP_DEV, 0)
            live = ((slots < REMOTE_DEV) | (slots - REMOTE_DEV < pair_count[owner])).astype(jnp.float32)
            live = live[None, None, :, None]
            x_local = jnp.take(rounded, local, axis=2)
            x_partner = jnp.take(rounded, partner, axis=2)
            term_i = complex_product('nqp,dnp->dnq', blocks, x_partner) * live
            term_j = complex_product('npq,dnp->dnq', blocks, x_local) * live
            total = total.at[:, :, local].add(term_i).at[:, :, partner].add(term_j)
            own_blocks = lax.dynamic_slice_in_dim(self_blocks, owner * CL_DEV, CL_DEV, 0)
            own_x = lax.dynamic_slice_in_dim(rounded, owner * CL_DEV, CL_DEV, 2)
            own_term = complex_product('cqp,dcp->dcq', own_blocks, own_x)
            previous = lax.dynamic_slice_in_dim(total, owner * CL_DEV, CL_DEV, 2)
            total = lax.dynamic_update_slice_in_dim(total, previous + own_term, owner * CL_DEV, 2)
            inward = lax.dynamic_slice_in_dim(far_in, owner * CL_DEV, CL_DEV, 0)
            rank = lax.dynamic_slice_in_dim(far_rank, owner * CL_DEV, CL_DEV, 0)
            mask = (ranks_axis[None, :] < rank[:, None]).astype(jnp.float32)
            contrib = complex_product('crp,dcp->dcr', inward, own_x) * mask[None, None]
            moments = moments + lax.optimization_barrier(jnp.sum(contrib, axis=2))
            return ((total, moments), None)
        start = (jnp.zeros(vec.shape, jnp.float32), jnp.zeros((2, NDIR, R), jnp.float32))
        (near, moments), _ = lax.scan(step, start, owners)

        def far_part(owner):
            outward = lax.dynamic_slice_in_dim(far_out, owner * CL_DEV, CL_DEV, 0)
            rank = lax.dynamic_slice_in_dim(far_rank, owner * CL_DEV, CL_DEV, 0)
            mask = (ranks_axis[None, :] < rank[:, None]).astype(jnp.float32)
            spread = lax.optimization_barrier((moments[:, :, None, :] * mask[None, None]).astype(jnp.bfloat16))
            return complex_product('crp,dcr->dcp', outward, spread)
        far = lax.map(far_part, owners)
        far = jnp.transpose(far, (1, 2, 0, 3, 4)).reshape(vec.shape)
        return vec + near + far
    start_vec = incident.reshape(2, NDIR, CLUSTERS, P_SIZE)
    beta = jnp.sqrt(lax.optimization_barrier(jnp.sum(start_vec * start_vec, axis=(0, 2, 3))))
    basis = [start_vec / beta[None, :, None, None]]
    zero = jnp.zeros((2, NDIR), jnp.float32)
    hess = [[zero for _ in range(ITERS)] for _ in range(ITERS + 1)]
    for step_k in range(ITERS):
        work = operate(basis[step_k])
        products = [inner(basis[j], work) for j in range(step_k + 1)]
        for j in range(step_k + 1):
            work = work - scale_by(products[j], basis[j])
            hess[j][step_k] = products[j]
        size = jnp.sqrt(lax.optimization_barrier(jnp.sum(work * work, axis=(0, 2, 3))))
        hess[step_k + 1][step_k] = jnp.stack([size, jnp.zeros_like(size)])
        if step_k + 1 < ITERS:
            basis.append(work / size[None, :, None, None])
    coeffs = least_squares(hess, beta)
    solution = jnp.zeros_like(start_vec)
    for k in range(ITERS):
        solution = solution + scale_by(coeffs[k], basis[k])
    intensity = lax.optimization_barrier(jnp.sum(solution * solution, axis=(0, 1))) / NDIR
    return (solution.reshape(2, NDIR, NPAN), intensity.reshape(NPAN))
```

```python
import functools

import jax
import jax.numpy as jnp
from jax import lax
from jax.experimental import pallas as pl
from jax.experimental.pallas import tpu as pltpu
from jax.sharding import PartitionSpec as P

NDIR = 128
ITERS = 3
REMOTE_DEV = 32
UNROLL = 8
F32 = jnp.float32
BF16 = jnp.bfloat16


def solve_small(matrix, vector):
    order = len(vector)
    rows = [list(line) for line in matrix]
    values = list(vector)
    for col in range(order):
        inverse = 1.0 / rows[col][col]
        for row in range(col + 1, order):
            factor = rows[row][col] * inverse
            for other in range(col + 1, order):
                rows[row][other] = rows[row][other] - factor * rows[col][other]
            values[row] = values[row] - factor * values[col]
    result = [None] * order
    for row in range(order - 1, -1, -1):
        total = values[row]
        for other in range(row + 1, order):
            total = total - rows[row][other] * result[other]
        result[row] = total / rows[row][row]
    return result


def least_squares(hess, beta):
    count = len(hess[0])
    g_real = [[None] * count for _ in range(count)]
    g_imag = [[None] * count for _ in range(count)]
    for first in range(count):
        for second in range(count):
            total_r = 0.0
            total_i = 0.0
            for row in range(min(first, second) + 2):
                ha = hess[row][first]
                hb = hess[row][second]
                total_r = total_r + ha[0] * hb[0] + ha[1] * hb[1]
                total_i = total_i + ha[0] * hb[1] - ha[1] * hb[0]
            g_real[first][second] = total_r
            g_imag[first][second] = total_i
    matrix = []
    for first in range(count):
        matrix.append(
            [g_real[first][b] for b in range(count)] + [-g_imag[first][b] for b in range(count)]
        )
    for first in range(count):
        matrix.append(
            [g_imag[first][b] for b in range(count)] + [g_real[first][b] for b in range(count)]
        )
    vector = [beta * hess[0][a][0] for a in range(count)] + [
        -beta * hess[0][a][1] for a in range(count)
    ]
    found = solve_small(matrix, vector)
    return [(found[a], found[a + count]) for a in range(count)]


def times(left, right):
    return lax.dot_general(left, right, (((1,), (0,)), ((), ())), preferred_element_type=F32)


def times_t(left, right):
    return lax.dot_general(left, right, (((1,), (1,)), ((), ())), preferred_element_type=F32)


def combine(by_real, by_imag):
    half = by_real.shape[0] // 2
    return jnp.concatenate(
        [by_real[:half] - by_imag[half:], by_real[half:] + by_imag[:half]], axis=0
    )


def forward(vec, block):
    panels = block.shape[1]
    both = times_t(vec, block)
    return combine(both[:, :panels], both[:, panels:])


def backward(vec, block):
    panels = block.shape[1]
    return combine(times(vec, block[:panels]), times(vec, block[panels:]))


def loop(first, last, step, carry=None, unroll=UNROLL):
    unroll = min(unroll, last - first)

    def several(number, state):
        for inner in range(unroll):
            state = step(first + number * unroll + inner, state)
        return state

    return lax.fori_loop(0, (last - first) // unroll, several, carry)


def kernel(geom, idx, rank, inc, pairs_hbm, selfs_hbm, fin, fout, out, inten, *scratch):
    n, nd, clusters, rim, dirs, panels, ranks, slots = geom
    near_slots = slots - REMOTE_DEV
    half_slots = near_slots // 2
    (
        pairs, selfs, win, wout, v0, v1, v2, vb, own, rimsum, tr,
        halo0, halo1, halo2, give0, give1, give2, take0, take1, take2,
        small_out, small_in, mom_out, mom_in, pow_out, pow_in,
        load_sem, small_s, small_r, mom_s, mom_r, halo_s, halo_r, give_s, give_r, pow_s, pow_r,
    ) = scratch
    basis = [v0, v1, v2]
    halos, gives, takes = [halo0, halo1, halo2], [give0, give1, give2], [take0, take1, take2]
    me = lax.axis_index("space")
    me_dir = lax.axis_index("dir")

    load_pairs = pltpu.make_async_copy(pairs_hbm, pairs, load_sem.at[0])
    load_selfs = pltpu.make_async_copy(selfs_hbm, selfs, load_sem.at[1])
    load_selfs.start()
    load_pairs.start()

    at_prev = 0
    at_last = at_prev + slots + near_slots
    at_mine = at_last + clusters
    at_part = at_mine + slots
    at_rprev = at_part + slots
    at_rlast = at_rprev + REMOTE_DEV

    barrier = pltpu.get_barrier_semaphore()
    for off in range(1, n):
        pl.semaphore_signal(
            barrier, inc=1, device_id={"space": lax.rem(me + off, n)},
            device_id_type=pl.DeviceIdType.MESH,
        )
    for off in range(1, nd):
        pl.semaphore_signal(
            barrier, inc=1, device_id={"dir": lax.rem(me_dir + off, nd)},
            device_id_type=pl.DeviceIdType.MESH,
        )

    @pl.when(me == 0)
    def _():
        for k in range(ITERS):
            halos[k][0:rim] = jnp.zeros((rim, 2 * dirs, panels), BF16)
            takes[k][0:rim] = jnp.zeros((rim, 2 * dirs, panels), BF16)

    @pl.when(me == n - 1)
    def _():
        for k in range(ITERS):
            halos[k][rim : 2 * rim] = jnp.zeros((rim, 2 * dirs, panels), BF16)
            takes[k][rim : 2 * rim] = jnp.zeros((rim, 2 * dirs, panels), BF16)

    rimsum[0] = jnp.zeros((2 * dirs, panels), F32)
    tr[...] = jnp.zeros(tr.shape, F32)
    lane = lax.broadcasted_iota(jnp.int32, (dirs, panels), 1)
    rank_row = lax.rem(lax.broadcasted_iota(jnp.int32, (2 * ranks, panels), 0), ranks)

    def remote(src, dst, send, recv, axis, target):
        return pltpu.make_async_remote_copy(
            src_ref=src, dst_ref=dst, send_sem=send, recv_sem=recv,
            device_id={axis: target}, device_id_type=pl.DeviceIdType.MESH,
        )

    def small_start(number, parts):
        packed = jnp.zeros((dirs, panels), F32)
        for place, part in enumerate(parts):
            packed = jnp.where(lane == place, jnp.sum(part, axis=1, keepdims=True), packed)
        tr[0:dirs] = packed
        small_out[number] = tr[...].T[0:8]
        copies = []
        for off in range(1, n):
            copy = remote(
                small_out.at[number], small_in.at[number, off - 1],
                small_s.at[number, off - 1], small_r.at[number, off - 1],
                "space", lax.rem(me + off, n),
            )
            copy.start()
            copies.append(copy)
        return copies

    def small_sum(number, parts):
        copies = small_start(number, parts)
        total = small_out[number]
        for off, copy in enumerate(copies):
            copy.wait_recv()
            total = total + small_in[number, off]
        for copy in copies:
            copy.wait_send()
        return [total[q : q + 1] for q in range(8)]

    def columns(rows):
        for place, row in enumerate(rows):
            tr[place : place + 1] = row
        turned = tr[...].T
        return [
            jnp.broadcast_to(turned[0:dirs, q : q + 1], (dirs, panels)) for q in range(len(rows))
        ]

    def norm_step(c, total):
        at = pl.ds(pl.multiple_of(c * panels, panels), panels)
        real, imag = inc[0, :, at], inc[1, :, at]
        return total + real * real + imag * imag

    partial = loop(0, clusters, norm_step, jnp.zeros((dirs, panels), F32))

    def mask_step(c, state):
        keep = (rank_row < rank[c]).astype(F32)
        win[c] = (fin[c].astype(F32) * keep).astype(BF16)
        wout[c] = (fout[c].astype(F32) * keep).astype(BF16)
        return state

    pl.semaphore_wait(barrier, n - 1 + nd - 1)
    beta = jnp.sqrt(small_sum(0, [partial])[0])
    loop(0, clusters, mask_step, 0)

    hess = [[None] * ITERS for _ in range(ITERS + 1)]
    zero_row = jnp.zeros((1, panels), F32)
    for row in range(ITERS + 1):
        for col in range(ITERS):
            hess[row][col] = (zero_row, zero_row)
    inverse_beta = columns([1.0 / beta])[0]
    scales = None
    loaded = False

    for k in range(ITERS):
        here = basis[k]

        def make_step(c, moments):
            if k == 0:
                at = pl.ds(pl.multiple_of(c * panels, panels), panels)
                vec = jnp.concatenate(
                    [inc[0, :, at] * inverse_beta, inc[1, :, at] * inverse_beta], axis=0
                )
            else:
                vec = here[c]
                real, imag = vec[:dirs], vec[dirs:]
                for j in range(k):
                    other = basis[j][c]
                    fr, fi = scales[2 * j], scales[2 * j + 1]
                    real = real - (fr * other[:dirs] - fi * other[dirs:])
                    imag = imag - (fr * other[dirs:] + fi * other[:dirs])
                vec = jnp.concatenate([real * scales[2 * k], imag * scales[2 * k]], axis=0)
            here[c] = vec
            rounded = vec.astype(BF16)
            vb[c] = rounded
            return moments + times_t(rounded, win[c])

        to_prev = remote(
            vb.at[0:rim], halos[k].at[rim : 2 * rim], halo_s.at[k, 0], halo_r.at[k, 1],
            "space", lax.rem(me + n - 1, n),
        )
        to_next = remote(
            vb.at[clusters - rim : clusters], halos[k].at[0:rim], halo_s.at[k, 1],
            halo_r.at[k, 0], "space", lax.rem(me + 1, n),
        )
        moments = jnp.zeros((2 * dirs, 2 * ranks), F32)
        moments = loop(0, rim, make_step, moments)

        @pl.when(me > 0)
        def _():
            to_prev.start()

        moments = loop(clusters - rim, clusters, make_step, moments)

        @pl.when(me < n - 1)
        def _():
            to_next.start()

        moments = loop(rim, clusters - rim, make_step, moments)
        mom_r_part = moments[:dirs, :ranks] - moments[dirs:, ranks:]
        mom_i_part = moments[:dirs, ranks:] + moments[dirs:, :ranks]
        mom_out[k] = jnp.concatenate([mom_r_part, mom_i_part], axis=1)
        mom_copies = []
        for off in range(1, n):
            copy = remote(
                mom_out.at[k], mom_in.at[k, off - 1], mom_s.at[k, off - 1],
                mom_r.at[k, off - 1], "space", lax.rem(me + off, n),
            )
            copy.start()
            mom_copies.append(copy)

        if not loaded:
            load_selfs.wait()
            load_pairs.wait()
            loaded = True

        def self_step(c, state):
            own[c] = forward(vb[c], selfs[c])
            return state

        def near_step(first_slot, first_place):
            def step(m, state):
                slot = first_slot + m
                place = first_place + 2 * m
                block = pairs[slot]
                fwd = forward(vb[idx[at_part + slot]], block)
                bwd = backward(vb[idx[at_mine + slot]], block)
                own[clusters + place] = own[idx[at_prev + place]] + fwd
                own[clusters + place + 1] = own[idx[at_prev + place + 1]] + bwd
                return state
            return step

        def remote_step(slot, state):
            place = 2 * half_slots + slot
            block = pairs[slot]
            bwd = backward(vb[idx[at_mine + slot]], block)
            fwd = forward(halos[k][idx[at_part + slot]], block)
            rimsum[1 + slot] = rimsum[idx[at_rprev + slot]] + bwd
            own[clusters + place] = own[idx[at_prev + place]] + fwd
            return state

        def give_step(t, state):
            gives[k][t] = rimsum[idx[at_rlast + t]].astype(BF16)
            return state

        loop(0, clusters, self_step, 0)
        loop(0, half_slots, near_step(REMOTE_DEV, 0), 0)

        @pl.when(me > 0)
        def _():
            to_next.wait_recv()

        @pl.when(me < n - 1)
        def _():
            to_prev.wait_recv()

        loop(0, REMOTE_DEV, remote_step, 0)
        loop(0, 2 * rim, give_step, 0)
        give_prev = remote(
            gives[k].at[0:rim], takes[k].at[rim : 2 * rim], give_s.at[k, 0], give_r.at[k, 1],
            "space", lax.rem(me + n - 1, n),
        )
        give_next = remote(
            gives[k].at[rim : 2 * rim], takes[k].at[0:rim], give_s.at[k, 1], give_r.at[k, 0],
            "space", lax.rem(me + 1, n),
        )

        @pl.when(me > 0)
        def _():
            give_prev.start()

        @pl.when(me < n - 1)
        def _():
            give_next.start()

        loop(
            0, half_slots,
            near_step(REMOTE_DEV + half_slots, 2 * half_slots + REMOTE_DEV), 0,
        )

        total = mom_out[k]
        for off, copy in enumerate(mom_copies):
            copy.wait_recv()
            total = total + mom_in[k, off]
        for copy in mom_copies:
            copy.wait_send()
        left, right = total[:, :ranks], total[:, ranks:]
        spread = jnp.concatenate(
            [
                jnp.concatenate([left, -right], axis=1),
                jnp.concatenate([right, left], axis=1),
            ],
            axis=0,
        ).astype(BF16)

        @pl.when(me > 0)
        def _():
            to_prev.wait_send()
            give_prev.wait_send()
            give_next.wait_recv()

        @pl.when(me < n - 1)
        def _():
            to_next.wait_send()
            give_next.wait_send()
            give_prev.wait_recv()

        def gather_step(shift):
            def step(c, sums):
                vec = own[idx[at_last + c]] + times(spread, wout[c])
                if shift is not None:
                    vec = vec + takes[k][c - shift].astype(F32)
                if k + 1 < ITERS:
                    basis[k + 1][c] = vec
                real, imag = vec[:dirs], vec[dirs:]
                result = []
                for j in range(k + 1):
                    other = basis[j][c]
                    br, bi = other[:dirs], other[dirs:]
                    result.append(sums[2 * j] + (br * real + bi * imag))
                    result.append(sums[2 * j + 1] + (br * imag - bi * real))
                result.append(sums[2 * k + 2] + (real * real + imag * imag))
                return tuple(result)
            return step

        sums = tuple(jnp.zeros((dirs, panels), F32) for _ in range(2 * k + 3))
        sums = loop(0, rim, gather_step(0), sums, 4)
        sums = loop(rim, clusters - rim, gather_step(None), sums, 4)
        sums = loop(clusters - rim, clusters, gather_step(clusters - 2 * rim), sums, 4)
        rows = small_sum(1 + k, sums)
        square = rows[2 * k + 2]
        rest = square
        for j in range(k + 1):
            rest = rest - (rows[2 * j] * rows[2 * j] + rows[2 * j + 1] * rows[2 * j + 1])
            shift = 1.0 if j == k else 0.0
            hess[j][k] = (rows[2 * j] + shift, rows[2 * j + 1])
        size = jnp.sqrt(jnp.maximum(rest, square * 1e-14))
        hess[k + 1][k] = (size, zero_row)
        if k + 1 < ITERS:
            scales = columns([rows[q] for q in range(2 * k + 2)] + [1.0 / size])

    coeffs = least_squares(hess, beta)
    factors = columns([part for pair in coeffs for part in pair])

    def final_step(c, state):
        real = imag = None
        for k in range(ITERS):
            vec = basis[k][c]
            br, bi = vec[:dirs], vec[dirs:]
            fr, fi = factors[2 * k], factors[2 * k + 1]
            add_r, add_i = fr * br - fi * bi, fr * bi + fi * br
            real = add_r if real is None else real + add_r
            imag = add_i if imag is None else imag + add_i
        at = pl.ds(pl.multiple_of(c * panels, panels), panels)
        out[0, :, at] = real
        out[1, :, at] = imag
        pow_out[pl.ds(c, 1)] = jnp.sum(real * real + imag * imag, axis=0, keepdims=True)
        return state

    loop(0, clusters, final_step, 0)
    copies = []
    for off in range(1, nd):
        copy = remote(
            pow_out, pow_in.at[off - 1], pow_s.at[off - 1], pow_r.at[off - 1],
            "dir", lax.rem(me_dir + off, nd),
        )
        copy.start()
        copies.append(copy)
    total = pow_out[...]
    for off, copy in enumerate(copies):
        copy.wait_recv()
        total = total + pow_in[off]
    inten[...] = total * (1.0 / NDIR)
    for copy in copies:
        copy.wait_send()


def plan(me, clusters, rim, pair_local, pair_partner, pair_count):
    slots = pair_local.shape[0]
    near_slots = slots - REMOTE_DEV
    half = near_slots // 2
    first = me * clusters
    partner = pair_partner - first
    side = jnp.clip(jnp.where(partner < 0, partner + rim, partner - clusters + rim), 0, 2 * rim - 1)
    near = jnp.arange(slots, dtype=jnp.int32) >= REMOTE_DEV
    part = jnp.where(near, jnp.clip(partner, 0, clusters - 1), side)
    live = jnp.arange(near_slots, dtype=jnp.int32) < pair_count[0]
    near_keys = jnp.stack([pair_local[REMOTE_DEV:], part[REMOTE_DEV:]], axis=1)
    near_keys = jnp.where(live[:, None], near_keys, -1)
    keys = jnp.concatenate(
        [near_keys[:half].reshape(-1), pair_local[:REMOTE_DEV], near_keys[half:].reshape(-1)]
    )

    def chain(keys, wanted, base, start_of):
        places = jnp.arange(keys.shape[0], dtype=jnp.int32)
        earlier = (keys[None, :] == keys[:, None]) & (places[None, :] < places[:, None])
        before = jnp.max(jnp.where(earlier, places[None, :] + base, start_of(keys)[:, None]), axis=1)
        goal = jnp.arange(wanted, dtype=jnp.int32)
        hit = keys[None, :] == goal[:, None]
        final = jnp.max(jnp.where(hit, places[None, :] + base, start_of(goal)[:, None]), axis=1)
        return before, final

    before, final = chain(keys, clusters, clusters, lambda key: jnp.maximum(key, 0))
    r_before, r_final = chain(part[:REMOTE_DEV], 2 * rim, 1, jnp.zeros_like)
    return jnp.concatenate([before, final, pair_local, part, r_before, r_final])


def body(
    n, nd,
    incident, pair_blocks, pair_local, pair_partner, pair_count,
    self_blocks, far_in, far_out, far_rank,
):
    clusters, _, panels, _ = self_blocks.shape
    ranks = far_in.shape[2]
    slots = pair_blocks.shape[0]
    dirs = incident.shape[1]
    rim = clusters // 4
    me = lax.axis_index("space")
    table = plan(me, clusters, rim, pair_local, pair_partner, pair_count)
    geom = (n, nd, clusters, rim, dirs, panels, ranks, slots)
    rows = 2 * dirs
    dma = pltpu.SemaphoreType.DMA
    vmem = pl.BlockSpec(memory_space=pltpu.VMEM)
    smem = pl.BlockSpec(memory_space=pltpu.SMEM)
    hbm = pl.BlockSpec(memory_space=pl.ANY)
    solution, intensity = pl.pallas_call(
        functools.partial(kernel, geom),
        out_shape=[
            jax.ShapeDtypeStruct(incident.shape, F32),
            jax.ShapeDtypeStruct((clusters, panels), F32),
        ],
        in_specs=[smem, smem, vmem, hbm, hbm, vmem, vmem],
        out_specs=[vmem, vmem],
        scratch_shapes=[
            pltpu.VMEM((slots, 2 * panels, panels), BF16),
            pltpu.VMEM((clusters, 2 * panels, panels), BF16),
            pltpu.VMEM((clusters, 2 * ranks, panels), BF16),
            pltpu.VMEM((clusters, 2 * ranks, panels), BF16),
        ]
        + [pltpu.VMEM((clusters, rows, panels), F32)] * ITERS
        + [
            pltpu.VMEM((clusters, rows, panels), BF16),
            pltpu.VMEM((clusters + 2 * slots - REMOTE_DEV, rows, panels), F32),
            pltpu.VMEM((REMOTE_DEV + 1, rows, panels), F32),
            pltpu.VMEM((panels, panels), F32),
        ]
        + [pltpu.VMEM((2 * rim, rows, panels), BF16)] * (3 * ITERS)
        + [
            pltpu.VMEM((ITERS + 1, 8, panels), F32),
            pltpu.VMEM((ITERS + 1, n - 1, 8, panels), F32),
            pltpu.VMEM((ITERS, dirs, 2 * ranks), F32),
            pltpu.VMEM((ITERS, n - 1, dirs, 2 * ranks), F32),
            pltpu.VMEM((clusters, panels), F32),
            pltpu.VMEM((nd - 1, clusters, panels), F32),
            dma((2,)),
            dma((ITERS + 1, n - 1)),
            dma((ITERS + 1, n - 1)),
            dma((ITERS, n - 1)),
            dma((ITERS, n - 1)),
            dma((ITERS, 2)),
            dma((ITERS, 2)),
            dma((ITERS, 2)),
            dma((ITERS, 2)),
            dma((nd - 1,)),
            dma((nd - 1,)),
        ],
        compiler_params=pltpu.CompilerParams(
            collective_id=0, has_side_effects=True, vmem_limit_bytes=48 * 1024 * 1024
        ),
    )(
        table,
        far_rank,
        incident,
        pair_blocks.reshape(slots, 2 * panels, panels),
        self_blocks.reshape(clusters, 2 * panels, panels),
        far_in.reshape(clusters, 2 * ranks, panels),
        far_out.reshape(clusters, 2 * ranks, panels),
    )
    return solution, intensity.reshape(clusters * panels)


def solution(mesh):
    return jax.shard_map(
        functools.partial(body, mesh.shape["space"], mesh.shape["dir"]),
        mesh=mesh,
        in_specs=(
            P(None, "dir", "space"),
            P("space", None, None, None),
            P("space"),
            P("space"),
            P("space"),
            P("space", None, None, None),
            P("space", None, None, None),
            P("space", None, None, None),
            P("space"),
        ),
        out_specs=(P(None, "dir", "space"), P("space")),
        check_vma=False,
    )
```

```python
import functools

import jax
import jax.numpy as jnp
from jax import lax
from jax.experimental import pallas as pl
from jax.experimental.pallas import tpu as pltpu
from jax.sharding import PartitionSpec as P

NDIR = 128
ITERS = 3
REMOTE_DEV = 32
UNROLL = 16
F32 = jnp.float32
BF16 = jnp.bfloat16


def solve_small(matrix, vector):
    order = len(vector)
    rows = [list(line) for line in matrix]
    values = list(vector)
    for col in range(order):
        inverse = 1.0 / rows[col][col]
        for row in range(col + 1, order):
            factor = rows[row][col] * inverse
            for other in range(col + 1, order):
                rows[row][other] = rows[row][other] - factor * rows[col][other]
            values[row] = values[row] - factor * values[col]
    result = [None] * order
    for row in range(order - 1, -1, -1):
        total = values[row]
        for other in range(row + 1, order):
            total = total - rows[row][other] * result[other]
        result[row] = total / rows[row][row]
    return result


def least_squares(hess, beta):
    count = len(hess[0])
    g_real = [[None] * count for _ in range(count)]
    g_imag = [[None] * count for _ in range(count)]
    for first in range(count):
        for second in range(count):
            total_r = 0.0
            total_i = 0.0
            for row in range(min(first, second) + 2):
                ha = hess[row][first]
                hb = hess[row][second]
                total_r = total_r + ha[0] * hb[0] + ha[1] * hb[1]
                total_i = total_i + ha[0] * hb[1] - ha[1] * hb[0]
            g_real[first][second] = total_r
            g_imag[first][second] = total_i
    matrix = []
    for first in range(count):
        matrix.append(
            [g_real[first][b] for b in range(count)] + [-g_imag[first][b] for b in range(count)]
        )
    for first in range(count):
        matrix.append(
            [g_imag[first][b] for b in range(count)] + [g_real[first][b] for b in range(count)]
        )
    vector = [beta * hess[0][a][0] for a in range(count)] + [
        -beta * hess[0][a][1] for a in range(count)
    ]
    found = solve_small(matrix, vector)
    return [(found[a], found[a + count]) for a in range(count)]


def times(left, right):
    return lax.dot_general(left, right, (((1,), (0,)), ((), ())), preferred_element_type=F32)


def times_t(left, right):
    return lax.dot_general(left, right, (((1,), (1,)), ((), ())), preferred_element_type=F32)


def combine(by_real, by_imag):
    half = by_real.shape[0] // 2
    return jnp.concatenate(
        [by_real[:half] - by_imag[half:], by_real[half:] + by_imag[:half]], axis=0
    )


def forward(vec, block):
    panels = block.shape[1]
    both = times_t(vec, block)
    return combine(both[:, :panels], both[:, panels:])


def backward(vec, block):
    panels = block.shape[1]
    return combine(times(vec, block[:panels]), times(vec, block[panels:]))


def loop(first, last, step, carry=None, unroll=UNROLL):
    unroll = min(unroll, last - first)

    def several(number, state):
        for inner in range(unroll):
            state = step(first + number * unroll + inner, state)
        return state

    return lax.fori_loop(0, (last - first) // unroll, several, carry)


def kernel(
    geom, local, partner, count, rank, inc_hbm, pairs_hbm, selfs_hbm, fin_hbm, fout_hbm,
    out, inten, *scratch,
):
    n, nd, clusters, rim, dirs, panels, ranks, slots = geom
    near_slots = slots - REMOTE_DEV
    half_slots = near_slots // 2
    (
        inc, pairs, selfs, win, wout, table, idx, v0, v1, v2, vb, own, rimsum, tr,
        halo0, halo1, halo2, give0, give1, give2, take0, take1, take2,
        small_out, small_in, mom_out, mom_in, pow_out, pow_in,
        load_sem, small_s, small_r, mom_s, mom_r, halo_s, halo_r, give_s, give_r, pow_s, pow_r,
    ) = scratch
    basis = [v0, v1, v2]
    halos, gives, takes = [halo0, halo1, halo2], [give0, give1, give2], [take0, take1, take2]
    me = lax.axis_index("space")
    me_dir = lax.axis_index("dir")

    loads = [
        pltpu.make_async_copy(src, dst, load_sem.at[number])
        for number, (src, dst) in enumerate(
            [
                (inc_hbm, inc), (fin_hbm, win), (fout_hbm, wout), (selfs_hbm, selfs),
                (pairs_hbm, pairs),
            ]
        )
    ]
    for load in loads:
        load.start()
    load_inc, load_in, load_out, load_selfs, load_pairs = loads
    load_table = pltpu.make_async_copy(table, idx, load_sem.at[len(loads)])

    barrier = pltpu.get_barrier_semaphore()
    for off in range(1, n):
        pl.semaphore_signal(
            barrier, inc=1, device_id={"space": lax.rem(me + off, n)},
            device_id_type=pl.DeviceIdType.MESH,
        )
    for off in range(1, nd):
        pl.semaphore_signal(
            barrier, inc=1, device_id={"dir": lax.rem(me_dir + off, nd)},
            device_id_type=pl.DeviceIdType.MESH,
        )

    @pl.when(me == 0)
    def _():
        for k in range(ITERS):
            halos[k][0:rim] = jnp.zeros((rim, 2 * dirs, panels), BF16)
            takes[k][0:rim] = jnp.zeros((rim, 2 * dirs, panels), BF16)

    @pl.when(me == n - 1)
    def _():
        for k in range(ITERS):
            halos[k][rim : 2 * rim] = jnp.zeros((rim, 2 * dirs, panels), BF16)
            takes[k][rim : 2 * rim] = jnp.zeros((rim, 2 * dirs, panels), BF16)

    rimsum[0] = jnp.zeros((2 * dirs, panels), F32)
    tr[...] = jnp.zeros(tr.shape, F32)
    lane = lax.broadcasted_iota(jnp.int32, (dirs, panels), 1)
    rank_row = lax.rem(lax.broadcasted_iota(jnp.int32, (2 * ranks, panels), 0), ranks)

    def remote(src, dst, send, recv, axis, target):
        return pltpu.make_async_remote_copy(
            src_ref=src, dst_ref=dst, send_sem=send, recv_sem=recv,
            device_id={axis: target}, device_id_type=pl.DeviceIdType.MESH,
        )

    def small_start(number, parts):
        packed = jnp.zeros((dirs, panels), F32)
        for place, part in enumerate(parts):
            packed = jnp.where(lane == place, jnp.sum(part, axis=1, keepdims=True), packed)
        tr[0:dirs] = packed
        small_out[number] = tr[...].T[0:8]
        copies = []
        for off in range(1, n):
            copy = remote(
                small_out.at[number], small_in.at[number, off - 1],
                small_s.at[number, off - 1], small_r.at[number, off - 1],
                "space", lax.rem(me + off, n),
            )
            copy.start()
            copies.append(copy)
        return copies

    def small_finish(number, copies):
        total = small_out[number]
        for off, copy in enumerate(copies):
            copy.wait_recv()
            total = total + small_in[number, off]
        for copy in copies:
            copy.wait_send()
        return [total[q : q + 1] for q in range(8)]

    def columns(rows):
        for place, row in enumerate(rows):
            tr[place : place + 1] = row
        turned = tr[...].T
        return [
            jnp.broadcast_to(turned[0:dirs, q : q + 1], (dirs, panels)) for q in range(len(rows))
        ]

    def make_table():
        spot = lax.broadcasted_iota(jnp.int32, (1, panels), 1)
        order = jnp.where(
            spot < REMOTE_DEV, spot + half_slots,
            jnp.where(spot < REMOTE_DEV + half_slots, spot - REMOTE_DEV, spot),
        )
        base = me * clusters

        def near_part(slot):
            return jnp.clip(partner[slot] - base, 0, clusters - 1)

        def side_part(slot):
            offset = partner[slot] - base
            return jnp.clip(
                jnp.where(offset < 0, offset + rim, offset - clusters + rim), 0, 2 * rim - 1
            )

        def key_step(part_of):
            def step(slot, keys):
                first, second = keys
                here = spot == slot
                return (
                    jnp.where(here, local[slot], first), jnp.where(here, part_of(slot), second)
                )
            return step

        none = jnp.full((1, panels), -1, jnp.int32)
        keys = loop(0, REMOTE_DEV, key_step(side_part), (none, none))
        key_i, parts = loop(REMOTE_DEV, slots, key_step(near_part), keys)
        live = (spot < REMOTE_DEV) | (spot - REMOTE_DEV < count[0])
        key_i = jnp.where(live, key_i, -1)
        key_j = jnp.where(live & (spot >= REMOTE_DEV), parts, -1)
        key_r = jnp.where(spot < REMOTE_DEV, parts, -1)

        def put(state, key, when, entry):
            prev_i, prev_j, last = state
            prev_i = jnp.where((key_i == key) & (2 * order > when), entry, prev_i)
            prev_j = jnp.where((key_j == key) & (2 * order + 1 > when), entry, prev_j)
            return prev_i, prev_j, jnp.where(spot == key, entry, last)

        def near_put(shift):
            def step(slot, state):
                alive = slot - REMOTE_DEV < count[0]
                when = 2 * (slot - shift)
                state = put(state, jnp.where(alive, local[slot], -2), when, clusters + slot)
                return put(
                    state, jnp.where(alive, near_part(slot), -2), when + 1, clusters + slots + slot
                )
            return step

        def remote_put(slot, state):
            chain, prev_r, last_r = state
            chain = put(chain, local[slot], 2 * (slot + half_slots), clusters + slot)
            key = side_part(slot)
            prev_r = jnp.where((key_r == key) & (spot > slot), 1 + slot, prev_r)
            return chain, prev_r, jnp.where(spot == key, 1 + slot, last_r)

        zeros = jnp.zeros((1, panels), jnp.int32)
        chain = (jnp.maximum(key_i, 0), jnp.maximum(key_j, 0), spot)
        chain = loop(REMOTE_DEV, REMOTE_DEV + half_slots, near_put(REMOTE_DEV), chain)
        chain, prev_r, last_r = loop(0, REMOTE_DEV, remote_put, (chain, zeros, zeros))
        chain = loop(REMOTE_DEV + half_slots, slots, near_put(0), chain)
        rows = [chain[0], chain[1], chain[2], parts, prev_r, last_r]
        for place, row in enumerate(rows):
            table[place : place + 1] = row

    def norm_step(c, total):
        at = pl.ds(pl.multiple_of(c * panels, panels), panels)
        real, imag = inc[0, :, at], inc[1, :, at]
        return total + real * real + imag * imag

    load_inc.wait()
    partial = loop(0, clusters, norm_step, jnp.zeros((dirs, panels), F32))

    def mask_step(c, state):
        keep = (rank_row < rank[c]).astype(F32)
        win[c] = (win[c].astype(F32) * keep).astype(BF16)
        wout[c] = (wout[c].astype(F32) * keep).astype(BF16)
        return state

    pl.semaphore_wait(barrier, n - 1 + nd - 1)
    flying = small_start(0, [partial])
    make_table()
    load_table.start()
    load_in.wait()
    load_out.wait()
    loop(0, clusters, mask_step, 0)
    load_table.wait()
    beta = jnp.sqrt(small_finish(0, flying)[0])

    hess = [[None] * ITERS for _ in range(ITERS + 1)]
    zero_row = jnp.zeros((1, panels), F32)
    for row in range(ITERS + 1):
        for col in range(ITERS):
            hess[row][col] = (zero_row, zero_row)
    inverse_beta = columns([1.0 / beta])[0]
    scales = None
    loaded = False

    for k in range(ITERS):
        here = basis[k]

        def make_step(c, moments):
            if k == 0:
                at = pl.ds(pl.multiple_of(c * panels, panels), panels)
                vec = jnp.concatenate(
                    [inc[0, :, at] * inverse_beta, inc[1, :, at] * inverse_beta], axis=0
                )
            else:
                vec = here[c]
                real, imag = vec[:dirs], vec[dirs:]
                for j in range(k):
                    other = basis[j][c]
                    fr, fi = scales[2 * j], scales[2 * j + 1]
                    real = real - (fr * other[:dirs] - fi * other[dirs:])
                    imag = imag - (fr * other[dirs:] + fi * other[:dirs])
                vec = jnp.concatenate([real * scales[2 * k], imag * scales[2 * k]], axis=0)
            here[c] = vec
            rounded = vec.astype(BF16)
            vb[c] = rounded
            return moments + times_t(rounded, win[c])

        to_prev = remote(
            vb.at[0:rim], halos[k].at[rim : 2 * rim], halo_s.at[k, 0], halo_r.at[k, 1],
            "space", lax.rem(me + n - 1, n),
        )
        to_next = remote(
            vb.at[clusters - rim : clusters], halos[k].at[0:rim], halo_s.at[k, 1],
            halo_r.at[k, 0], "space", lax.rem(me + 1, n),
        )
        moments = jnp.zeros((2 * dirs, 2 * ranks), F32)
        moments = loop(0, rim, make_step, moments)

        @pl.when(me > 0)
        def _():
            to_prev.start()

        moments = loop(clusters - rim, clusters, make_step, moments)

        @pl.when(me < n - 1)
        def _():
            to_next.start()

        moments = loop(rim, clusters - rim, make_step, moments)
        mom_r_part = moments[:dirs, :ranks] - moments[dirs:, ranks:]
        mom_i_part = moments[:dirs, ranks:] + moments[dirs:, :ranks]
        mom_out[k] = jnp.concatenate([mom_r_part, mom_i_part], axis=1)
        mom_copies = []
        for off in range(1, n):
            copy = remote(
                mom_out.at[k], mom_in.at[k, off - 1], mom_s.at[k, off - 1],
                mom_r.at[k, off - 1], "space", lax.rem(me + off, n),
            )
            copy.start()
            mom_copies.append(copy)

        if not loaded:
            load_selfs.wait()
            load_pairs.wait()
            loaded = True

        def self_step(c, state):
            own[c] = forward(vb[c], selfs[c])
            return state

        def near_step(first_slot):
            def step(m, state):
                slot = first_slot + m
                block = pairs[slot]
                fwd = forward(vb[idx[3, slot]], block)
                bwd = backward(vb[local[slot]], block)
                own[clusters + slot] = own[idx[0, slot]] + fwd
                own[clusters + slots + slot] = own[idx[1, slot]] + bwd
                return state
            return step

        def remote_step(slot, state):
            block = pairs[slot]
            bwd = backward(vb[local[slot]], block)
            fwd = forward(halos[k][idx[3, slot]], block)
            rimsum[1 + slot] = rimsum[idx[4, slot]] + bwd
            own[clusters + slot] = own[idx[0, slot]] + fwd
            return state

        def give_step(t, state):
            gives[k][t] = rimsum[idx[5, t]].astype(BF16)
            return state

        loop(0, clusters, self_step, 0)
        loop(0, half_slots, near_step(REMOTE_DEV), 0)

        @pl.when(me > 0)
        def _():
            to_next.wait_recv()

        @pl.when(me < n - 1)
        def _():
            to_prev.wait_recv()

        loop(0, REMOTE_DEV, remote_step, 0)
        loop(0, 2 * rim, give_step, 0)
        give_prev = remote(
            gives[k].at[0:rim], takes[k].at[rim : 2 * rim], give_s.at[k, 0], give_r.at[k, 1],
            "space", lax.rem(me + n - 1, n),
        )
        give_next = remote(
            gives[k].at[rim : 2 * rim], takes[k].at[0:rim], give_s.at[k, 1], give_r.at[k, 0],
            "space", lax.rem(me + 1, n),
        )

        @pl.when(me > 0)
        def _():
            give_prev.start()

        @pl.when(me < n - 1)
        def _():
            give_next.start()

        loop(
            0, half_slots,
            near_step(REMOTE_DEV + half_slots), 0,
        )

        total = mom_out[k]
        for off, copy in enumerate(mom_copies):
            copy.wait_recv()
            total = total + mom_in[k, off]
        for copy in mom_copies:
            copy.wait_send()
        left, right = total[:, :ranks], total[:, ranks:]
        spread = jnp.concatenate(
            [
                jnp.concatenate([left, -right], axis=1),
                jnp.concatenate([right, left], axis=1),
            ],
            axis=0,
        ).astype(BF16)

        @pl.when(me > 0)
        def _():
            to_prev.wait_send()
            give_prev.wait_send()
            give_next.wait_recv()

        @pl.when(me < n - 1)
        def _():
            to_next.wait_send()
            give_next.wait_send()
            give_prev.wait_recv()

        def gather_step(shift):
            def step(c, sums):
                vec = own[idx[2, c]] + times(spread, wout[c])
                if shift is not None:
                    vec = vec + takes[k][c - shift].astype(F32)
                if k + 1 < ITERS:
                    basis[k + 1][c] = vec
                real, imag = vec[:dirs], vec[dirs:]
                result = []
                for j in range(k + 1):
                    other = basis[j][c]
                    br, bi = other[:dirs], other[dirs:]
                    result.append(sums[2 * j] + (br * real + bi * imag))
                    result.append(sums[2 * j + 1] + (br * imag - bi * real))
                result.append(sums[2 * k + 2] + (real * real + imag * imag))
                return tuple(result)
            return step

        sums = tuple(jnp.zeros((dirs, panels), F32) for _ in range(2 * k + 3))
        sums = loop(0, rim, gather_step(0), sums, 4)
        sums = loop(rim, clusters - rim, gather_step(None), sums, 4)
        sums = loop(clusters - rim, clusters, gather_step(clusters - 2 * rim), sums, 4)
        rows = small_finish(1 + k, small_start(1 + k, sums))
        square = rows[2 * k + 2]
        rest = square
        for j in range(k + 1):
            rest = rest - (rows[2 * j] * rows[2 * j] + rows[2 * j + 1] * rows[2 * j + 1])
            shift = 1.0 if j == k else 0.0
            hess[j][k] = (rows[2 * j] + shift, rows[2 * j + 1])
        size = jnp.sqrt(jnp.maximum(rest, square * 1e-14))
        hess[k + 1][k] = (size, zero_row)
        if k + 1 < ITERS:
            scales = columns([rows[q] for q in range(2 * k + 2)] + [1.0 / size])

    coeffs = least_squares(hess, beta)
    factors = columns([part for pair in coeffs for part in pair])

    def final_step(c, state):
        real = imag = None
        for k in range(ITERS):
            vec = basis[k][c]
            br, bi = vec[:dirs], vec[dirs:]
            fr, fi = factors[2 * k], factors[2 * k + 1]
            add_r, add_i = fr * br - fi * bi, fr * bi + fi * br
            real = add_r if real is None else real + add_r
            imag = add_i if imag is None else imag + add_i
        at = pl.ds(pl.multiple_of(c * panels, panels), panels)
        out[0, :, at] = real
        out[1, :, at] = imag
        pow_out[pl.ds(c, 1)] = jnp.sum(real * real + imag * imag, axis=0, keepdims=True)
        return state

    loop(0, clusters, final_step, 0)
    copies = []
    for off in range(1, nd):
        copy = remote(
            pow_out, pow_in.at[off - 1], pow_s.at[off - 1], pow_r.at[off - 1],
            "dir", lax.rem(me_dir + off, nd),
        )
        copy.start()
        copies.append(copy)
    total = pow_out[...]
    for off, copy in enumerate(copies):
        copy.wait_recv()
        total = total + pow_in[off]
    inten[...] = total * (1.0 / NDIR)
    for copy in copies:
        copy.wait_send()


def body(
    n, nd,
    incident, pair_blocks, pair_local, pair_partner, pair_count,
    self_blocks, far_in, far_out, far_rank,
):
    clusters, _, panels, _ = self_blocks.shape
    ranks = far_in.shape[2]
    slots = pair_blocks.shape[0]
    dirs = incident.shape[1]
    rim = clusters // 4
    geom = (n, nd, clusters, rim, dirs, panels, ranks, slots)
    rows = 2 * dirs
    dma = pltpu.SemaphoreType.DMA
    vmem = pl.BlockSpec(memory_space=pltpu.VMEM)
    smem = pl.BlockSpec(memory_space=pltpu.SMEM)
    hbm = pl.BlockSpec(memory_space=pl.ANY)
    solution, intensity = pl.pallas_call(
        functools.partial(kernel, geom),
        out_shape=[
            jax.ShapeDtypeStruct(incident.shape, F32),
            jax.ShapeDtypeStruct((clusters, panels), F32),
        ],
        in_specs=[smem] * 4 + [hbm] * 5,
        out_specs=[vmem, vmem],
        scratch_shapes=[
            pltpu.VMEM(incident.shape, F32),
            pltpu.VMEM((slots, 2 * panels, panels), BF16),
            pltpu.VMEM((clusters, 2 * panels, panels), BF16),
            pltpu.VMEM((clusters, 2 * ranks, panels), BF16),
            pltpu.VMEM((clusters, 2 * ranks, panels), BF16),
            pltpu.VMEM((8, panels), jnp.int32),
            pltpu.SMEM((8, panels), jnp.int32),
        ]
        + [pltpu.VMEM((clusters, rows, panels), F32)] * ITERS
        + [
            pltpu.VMEM((clusters, rows, panels), BF16),
            pltpu.VMEM((clusters + 2 * slots, rows, panels), F32),
            pltpu.VMEM((REMOTE_DEV + 1, rows, panels), F32),
            pltpu.VMEM((panels, panels), F32),
        ]
        + [pltpu.VMEM((2 * rim, rows, panels), BF16)] * (3 * ITERS)
        + [
            pltpu.VMEM((ITERS + 1, 8, panels), F32),
            pltpu.VMEM((ITERS + 1, n - 1, 8, panels), F32),
            pltpu.VMEM((ITERS, dirs, 2 * ranks), F32),
            pltpu.VMEM((ITERS, n - 1, dirs, 2 * ranks), F32),
            pltpu.VMEM((clusters, panels), F32),
            pltpu.VMEM((nd - 1, clusters, panels), F32),
            dma((6,)),
            dma((ITERS + 1, n - 1)),
            dma((ITERS + 1, n - 1)),
            dma((ITERS, n - 1)),
            dma((ITERS, n - 1)),
            dma((ITERS, 2)),
            dma((ITERS, 2)),
            dma((ITERS, 2)),
            dma((ITERS, 2)),
            dma((nd - 1,)),
            dma((nd - 1,)),
        ],
        compiler_params=pltpu.CompilerParams(
            collective_id=0, has_side_effects=True, vmem_limit_bytes=60 * 1024 * 1024
        ),
    )(
        pair_local,
        pair_partner,
        pair_count,
        far_rank,
        incident,
        pair_blocks.reshape(slots, 2 * panels, panels),
        self_blocks.reshape(clusters, 2 * panels, panels),
        far_in.reshape(clusters, 2 * ranks, panels),
        far_out.reshape(clusters, 2 * ranks, panels),
    )
    return solution, intensity.reshape(clusters * panels)


def solution(mesh):
    return jax.shard_map(
        functools.partial(body, mesh.shape["space"], mesh.shape["dir"]),
        mesh=mesh,
        in_specs=(
            P(None, "dir", "space"),
            P("space", None, None, None),
            P("space"),
            P("space"),
            P("space"),
            P("space", None, None, None),
            P("space", None, None, None),
            P("space", None, None, None),
            P("space"),
        ),
        out_specs=(P(None, "dir", "space"), P("space")),
        check_vma=False,
    )
```
